128 devices in a mesh: patch: 16 (over z, x_hi, core), head: 8 (over x_lo, y).
Axes of the slice: x: 4 (x_hi: 2, x_lo: 2; x = x_hi * 2 + x_lo), y: 4, z: 4, core: 2. Of those that a mesh axis runs over, the one named last changes fastest.
Arguments:
- hidden_in: bfloat16 [8192, 5120], P('patch', 'head'), may hold values from -6 to 6
- positions: int32 [8192], P('patch'), may hold values from 0 to 8191, each once
- modulation: float32 [3, 5120], replicated, may hold values from -4 to 4
- w_qkv: bfloat16 [5120, 3, 3072], P(None, None, 'head'), may hold values from -1 to 1
- qk_gain: float32 [2, 3072], P(None, 'head'), may hold values from 1.5 to 4
- w_out: bfloat16 [3072, 5120], P('head'), may hold values from -0.109375 to 0.109375
- stale_kv: bfloat16 [8192, 2, 3072], P('patch', None, 'head'), may hold values from -500 to 500
Outputs:
- hidden_out: bfloat16 [8192, 5120], P('patch', 'head')
The draws below stay inside these ranges and needn't reach their ends.
Inputs may be any that keep to these rules, and one draw needn't show every extreme that they name: `positions`: every position of 0 to 8191 is held by exactly one row.
All inputs are finite; a program needn't handle non-finite values.
Results may differ from the reference program's by a relative error of at most 0.02.
The reference program's roundings to bfloat16 on the way count: a program that leaves them out, or rounds other values in their place, can miss the bound.
Values may be sent and summed in bfloat16 or wider, within the bound.
A program may use at most 192 MiB of HBM per device.

```python
import math
import jax
import jax.numpy as jnp
from jax import lax

D = 5120
HD = 128
HEADS = 24
TOK_DEV = 512
TOKENS = 8192
N_PATCH = 16
N_HEAD = 8


def draw_w_qkv(key, part):
    key = jax.random.fold_in(key, 11)
    key_one, key_two = jax.random.split(key)
    full_width = HEADS * HD
    base_draw = jax.random.normal(key_one, (D, 3, full_width), jnp.float32) * D ** (-0.5)
    column_scale = jnp.exp(jax.random.uniform(key_two, (3, full_width), jnp.float32, math.log(0.7), math.log(1.4)))
    head_ids = (jnp.arange(full_width) // HD).astype(jnp.float32)
    rising = 4.0 ** (0.5 * head_ids / (HEADS - 1))
    return jnp.clip(base_draw * column_scale * rising[None, None, :], -1.0, 1.0).astype(jnp.bfloat16)


def draw_stale_kv(key, part):
    key = jax.random.fold_in(key, 23)
    subkeys = jax.random.split(key, 2)
    full_width = HEADS * HD
    key_part = jax.random.normal(subkeys[0], (TOKENS, full_width), jnp.float32) * 2.5
    value_part = jax.random.normal(subkeys[1], (TOKENS, full_width), jnp.float32)
    return jnp.stack([key_part, value_part], axis=1).astype(jnp.bfloat16)


def block_scale(own_key, extent, pieces, smallest, top_value):
    def one(axis_at, blocks):
        draws = jax.random.uniform(jax.random.fold_in(jax.random.fold_in(own_key, 6), axis_at), (blocks,), jnp.float32, smallest / len(pieces), top_value / len(pieces))
        return jnp.repeat(jnp.exp(draws), extent[axis_at] // blocks).reshape((-1,) + (1,) * (len(extent) - axis_at - 1))

    loudness = one(*pieces[0])
    for cut in pieces[1:]:
        loudness = loudness * one(*cut)
    return loudness


def scatter_about(rng, dims, deviation, reach, cuts=(), kind=jnp.bfloat16):
    entries = jax.random.normal(rng, dims, jnp.float32) * deviation
    if len(cuts) > 0:
        entries = block_scale(rng, dims, cuts, -0.22, 0.18) * entries
    return jnp.clip(entries, min=-reach, max=reach).astype(kind)


def setup_inputs(seed: int = 0) -> dict:
    key_of = jax.random.split(jax.random.key(seed), 8)
    hidden_in = scatter_about(key_of[0], (TOKENS, D), 1.0, 6.0, ((0, 16), (1, 8)))
    positions = jax.random.permutation(key_of[1], TOKENS).astype(jnp.int32)
    modulation = scatter_about(key_of[2], (3, D), 1.0, 4.0, (), jnp.float32)
    w_qkv = draw_w_qkv(jax.random.fold_in(key_of[7], 71), 0)
    qk_gain = jnp.clip(jnp.exp(math.log(4.0) - 0.98082925 * jax.random.uniform(key_of[4], (2, HEADS * HD), jnp.float32) ** block_scale(key_of[4], (2, HEADS * HD), ((1, 8),), -0.2, 0.2)), 1.5, 4.0)
    w_out = scatter_about(key_of[5], (HEADS * HD, D), (HEADS * HD) ** -0.5, 0.109375, ((0, 8),))
    stale_kv = draw_stale_kv(jax.random.fold_in(key_of[7], 71), 0)
    return {"hidden_in": hidden_in, "positions": positions, "modulation": modulation, "w_qkv": w_qkv, "qk_gain": qk_gain, "w_out": w_out, "stale_kv": stale_kv}


def rotate_pairs(values_in, positions):
    half_dim = values_in.shape[-1] // 2
    inverse_freq = 10000.0 ** (-2.0 * jnp.arange(half_dim, dtype=jnp.float32) / values_in.shape[-1])
    angles = positions.astype(jnp.float32)[:, None] * inverse_freq[None, :]
    cosine = jnp.cos(angles)[:, None, :]
    sine_part = jnp.sin(angles)[:, None, :]
    first_half = values_in[..., :half_dim]
    second_half = values_in[..., half_dim:]
    return jnp.concatenate([first_half * cosine - second_half * sine_part, first_half * sine_part + second_half * cosine], axis=-1)

def reference(hidden_in, positions, modulation, w_qkv, qk_gain, w_out, stale_kv):
    features = hidden_in.astype(jnp.float32)
    centered = features - lax.optimization_barrier(jnp.mean(features, axis=-1, keepdims=True))
    variance = lax.optimization_barrier(jnp.mean(centered * centered, axis=-1, keepdims=True))
    modulated = (centered * lax.rsqrt(variance + 1e-06) * (1.0 + modulation[1]) + modulation[0]).astype(jnp.bfloat16)
    full_width = HEADS * HD
    projected = jnp.dot(modulated, w_qkv.reshape(D, 3 * full_width), preferred_element_type=jnp.float32).reshape(TOKENS, 3, full_width)
    queries = projected[:, 0]
    keys_all = projected[:, 1]
    fresh_values = projected[:, 2].astype(jnp.bfloat16)
    queries = queries * lax.rsqrt(lax.optimization_barrier(jnp.mean(queries * queries, axis=-1, keepdims=True)) + 1e-06) * qk_gain[0]
    keys_all = keys_all * lax.rsqrt(lax.optimization_barrier(jnp.mean(keys_all * keys_all, axis=-1, keepdims=True)) + 1e-06) * qk_gain[1]
    rotated_queries = rotate_pairs(queries.reshape(TOKENS, HEADS, HD), positions).astype(jnp.bfloat16)
    rotated_keys = rotate_pairs(keys_all.reshape(TOKENS, HEADS, HD), positions).astype(jnp.bfloat16)
    fresh_table = jnp.stack([rotated_keys.reshape(TOKENS, full_width), fresh_values], axis=1)

    def one_patch(patch_index):
        first_row = (patch_index * TOK_DEV).astype(jnp.int32)
        own_rows = lax.dynamic_slice_in_dim(fresh_table, first_row, TOK_DEV, 0)
        table = lax.dynamic_update_slice(stale_kv, own_rows, (first_row, jnp.int32(0), jnp.int32(0)))
        query_rows = lax.dynamic_slice_in_dim(rotated_queries, first_row, TOK_DEV, 0).astype(jnp.float32)
        key_rows = table[:, 0].reshape(TOKENS, HEADS, HD).astype(jnp.float32)
        value_rows = table[:, 1].reshape(TOKENS, HEADS, HD).astype(jnp.float32)
        scores = jnp.einsum('qhd,khd->qhk', query_rows, key_rows) * HD ** (-0.5)
        row_max = lax.optimization_barrier(jnp.max(scores, axis=-1, keepdims=True))
        weights = jnp.exp(scores - row_max)
        totals = lax.optimization_barrier(jnp.sum(weights, axis=-1))
        rounded = lax.optimization_barrier(weights.astype(jnp.bfloat16)).astype(jnp.float32)
        attended = jnp.einsum('qhk,khd->qhd', rounded, value_rows) / totals[..., None]
        return attended.astype(jnp.bfloat16).reshape(TOK_DEV, full_width)
    attended = lax.map(one_patch, jnp.arange(N_PATCH, dtype=jnp.int32)).reshape(TOKENS, full_width)
    group_width = full_width // N_HEAD
    attention_out = jnp.zeros((TOKENS, D), jnp.float32)
    for group in range(N_HEAD):
        partial_term = jnp.dot(attended[:, group * group_width:(group + 1) * group_width], w_out[group * group_width:(group + 1) * group_width], preferred_element_type=jnp.float32).astype(jnp.bfloat16)
        attention_out = attention_out + lax.optimization_barrier(partial_term).astype(jnp.float32)
    return (features + modulation[2] * attention_out).astype(jnp.bfloat16)
```

```python
import functools
import math

import jax
import jax.numpy as jnp
from jax import lax
from jax.experimental import pallas as pl
from jax.experimental.pallas import tpu as pltpu
from jax.sharding import PartitionSpec as P

HD = 128
HEADS_DEV = 3
MODEL = 5120
COLS = 640
ROWS = 512
WIDTH = 384
FULL = 3072
TILE = 256
EXP_SCALE = HD ** (-0.5) * math.log2(math.e)
MESH = pl.DeviceIdType.MESH
NT = (((1,), (1,)), ((), ()))
PEERS = (6, 2, 5, 7, 1, 3, 4)


def dot(left, right):
    return jnp.dot(left, right, preferred_element_type=jnp.float32)


def dot_nt(left, right):
    return lax.dot_general(left, right, NT, preferred_element_type=jnp.float32)


def mirrored(rel):
    return 4 * (rel // 4) + (4 - rel % 4) % 4


def to_rows(columns):
    lane = lax.broadcasted_iota(jnp.int32, (ROWS, 128), 1)
    wide = jnp.where(lane == 0, columns[0], jnp.where(lane == 1, columns[1], 0.0))
    return wide.T[:8]


def to_columns(first, second):
    sub = lax.broadcasted_iota(jnp.int32, (128, ROWS), 0)
    tall = jnp.where(sub == 0, first, jnp.where(sub == 1, second, 0.0)).T
    return (
        jnp.broadcast_to(tall[:, 0:1], (ROWS, 128)),
        jnp.broadcast_to(tall[:, 1:2], (ROWS, 128)),
    )


def kernel(
    hid_in, ang, modulation, w_in, gain, wout_in, kv_in, out,
    hid, w, kv, wo, att, acc, q, cosine, sine, mean, rstd, stats, norms,
    own_stats, own_norms, run_max, run_sum, run_acc, score, total, send, recv, local,
):
    patch, head = lax.axis_index("patch"), lax.axis_index("head")
    z, xh, core = patch // 4, (patch // 2) % 2, patch % 2
    xl, y = head // 4, head % 4
    count = [0]
    copies = []

    def place(dz=0, dxh=0, dcore=0, rel=0):
        to_patch = ((z + dz) % 4) * 4 + ((xh + dxh) % 2) * 2 + (core + dcore) % 2
        to_head = ((xl + rel // 4) % 2) * 4 + (y + rel % 4) % 4
        return (to_patch, to_head)

    def ship(src, dst, to):
        i = count[0]
        count[0] += 1
        copy = pltpu.make_async_remote_copy(
            src_ref=src, dst_ref=dst, send_sem=send.at[i], recv_sem=recv.at[i],
            device_id=to, device_id_type=MESH,
        )
        copy.start()
        copies.append(copy)
        return copy

    load_hid = pltpu.make_async_copy(hid_in, hid.at[0], local.at[0])
    load_hid.start()
    load_w = pltpu.make_async_copy(w_in, w, local.at[1])
    load_w.start()
    own_cols = pl.ds(pl.multiple_of(head * COLS, COLS), COLS)
    load_wo = pltpu.make_async_copy(wout_in.at[:, own_cols], wo.at[0], local.at[2])
    load_wo.start()

    partners = [place(rel=r) for r in PEERS]
    partners += [place(dz=1), place(dz=3), place(dxh=1), place(dcore=1)]
    barrier = pltpu.get_barrier_semaphore()
    for to in partners:
        pl.semaphore_signal(barrier, inc=1, device_id=to, device_id_type=MESH)
    pl.semaphore_wait(barrier, len(partners))

    part = lambda t: pl.ds(t * TILE, TILE)
    near = {}
    for t in range(2):
        for rel in (1, 3, 4):
            near[rel, t] = ship(
                hid_in.at[part(t)], hid.at[mirrored(rel), part(t)], place(rel=rel)
            )
    kv_own = {
        dz: ship(kv_in, kv.at[((4 - dz) % 4) * 4], place(dz=dz)) for dz in (1, 3)
    }
    kv_core = [ship(kv_in, kv.at[1], place(dcore=1))]

    def pass_to_core(slot):
        kv_core.append(ship(kv.at[slot], kv.at[slot + 1], place(dcore=1)))

    load_hid.wait()
    own = hid[0].astype(jnp.float32)
    own_sum = jnp.sum(own, axis=1, keepdims=True)
    off = own - own_sum * (1.0 / COLS)
    own_stats[...] = to_rows((own_sum, jnp.sum(off * off, axis=1, keepdims=True)))
    stat_copies = [
        ship(own_stats, stats.at[mirrored(r)], place(rel=r)) for r in PEERS
    ]
    stats[0] = own_stats[...]

    angles = ang[...]
    lane = lax.broadcasted_iota(jnp.int32, (ROWS, HD), 1)
    cosine[...] = jnp.cos(angles)
    sine[...] = jnp.where(lane < HD // 2, -1.0, 1.0) * jnp.sin(angles)

    for copy in stat_copies:
        copy.wait_recv()
    sums = sum(stats[r, 0:1, :] for r in range(8))
    mean_row = sums * (1.0 / MODEL)
    squares = sum(
        stats[r, 1:2, :] + COLS * jnp.square(stats[r, 0:1, :] * (1.0 / COLS) - mean_row)
        for r in range(8)
    )
    mean[...], rstd[...] = to_columns(mean_row, lax.rsqrt(squares * (1.0 / MODEL) + 1e-6))
    load_w.wait()

    def project(rel, t, first=False):
        rows = slice(t * TILE, t * TILE + TILE)
        block = ((xl + rel // 4) % 2) * 4 + (y + rel % 4) % 4
        at = pl.ds(pl.multiple_of(block * COLS, COLS), COLS)
        features = hid[rel, rows].astype(jnp.float32)
        centre = jnp.concatenate([mean[rows]] * (COLS // 128), axis=1)
        factor = jnp.concatenate([rstd[rows]] * (COLS // 128), axis=1)
        shift, scale = modulation[0:1, at], modulation[1:2, at]
        modulated = ((features - centre) * factor * (1.0 + scale) + shift).astype(jnp.bfloat16)
        for j in range(3):
            cols = slice(j * WIDTH, j * WIDTH + WIDTH)
            term = dot(modulated, w[j, at, :])
            if first:
                acc[rows, cols] = term
            else:
                acc[rows, cols] += term

    for t in range(2):
        project(0, t, first=True)

    QUARTER = TILE // 2
    far, fwd, opp = {}, {}, {}
    for t in range(2):
        near[1, t].wait_recv()
        near[3, t].wait_recv()
        low, high = pl.ds(t * TILE, QUARTER), pl.ds(t * TILE + QUARTER, QUARTER)
        far[t] = (
            ship(hid.at[3, low], hid.at[2, low], place(rel=1)),
            ship(hid.at[1, high], hid.at[2, high], place(rel=3)),
        )
        near[4, t].wait_recv()
        fwd[t] = (
            ship(hid.at[4, part(t)], hid.at[7, part(t)], place(rel=1)),
            ship(hid.at[4, part(t)], hid.at[5, part(t)], place(rel=3)),
        )
        if t == 1:
            kv_x = ship(kv_in, kv.at[2], place(dxh=1))
        for rel in (1, 3, 4):
            project(rel, t)
    kv_own[1].wait_recv()
    kv_own[3].wait_recv()
    kv_far = [
        ship(kv.at[12, 0], kv.at[8, 0], place(dz=1)),
        ship(kv.at[4, 1], kv.at[8, 1], place(dz=3)),
    ]
    pass_to_core(12)
    pass_to_core(4)
    for t in range(2):
        for copy in far[t]:
            copy.wait_recv()
        opp[t] = ship(hid.at[2, part(t)], hid.at[6, part(t)], place(rel=4))
        project(2, t)
    for copy in fwd[0]:
        copy.wait_recv()
    project(5, 0)
    project(7, 0)
    kv_x.wait_recv()
    kv_x_own = [
        ship(kv.at[2], kv.at[14], place(dz=1)),
        ship(kv.at[2], kv.at[6], place(dz=3)),
    ]
    pass_to_core(2)
    for copy in fwd[1]:
        copy.wait_recv()
    project(5, 1)
    project(7, 1)
    for t in range(2):
        opp[t].wait_recv()
        project(6, t)

    queries, keys = acc[:, :WIDTH], acc[:, WIDTH : 2 * WIDTH]
    own_norms[...] = to_rows(
        (
            jnp.sum(queries * queries, axis=1, keepdims=True),
            jnp.sum(keys * keys, axis=1, keepdims=True),
        )
    )
    norm_copies = [
        ship(own_norms, norms.at[mirrored(r)], place(rel=r)) for r in PEERS
    ]
    norms[0] = own_norms[...]
    half = pl.ds(pl.multiple_of(core * (WIDTH // 2), WIDTH // 2), WIDTH // 2)
    wo_copies = {}
    for r in PEERS:
        to = place(rel=r)
        cols = pl.ds(pl.multiple_of(to[1] * COLS, COLS), COLS)
        wo_copies[mirrored(r)] = ship(wout_in.at[half, cols], wo.at[mirrored(r), half], to)
    kv[0, 1] = acc[:, 2 * WIDTH :].astype(jnp.bfloat16)
    for copy in norm_copies:
        copy.wait_recv()
    q_row, k_row = (
        lax.rsqrt(sum(norms[r, i : i + 1, :] for r in range(8)) * (1.0 / FULL) + 1e-6)
        for i in range(2)
    )
    q_factor, k_factor = to_columns(q_row, k_row)
    for h in range(HEADS_DEV):
        for i, factor in ((0, q_factor), (1, k_factor)):
            cols = slice(h * HD, h * HD + HD)
            value = acc[:, i * WIDTH + h * HD : i * WIDTH + h * HD + HD] * factor * gain[i : i + 1, cols]
            turned = (
                value * cosine[...] + pltpu.roll(value, HD // 2, 1) * sine[...]
            ).astype(jnp.bfloat16)
            if i == 0:
                q[h] = turned
            else:
                kv[0, 0, :, cols] = turned

    for copy in kv_far:
        copy.wait_recv()
    pass_to_core(8)
    for copy in kv_x_own:
        copy.wait_recv()
    kv_x_far = [
        ship(kv.at[14, 0], kv.at[10, 0], place(dz=1)),
        ship(kv.at[6, 1], kv.at[10, 1], place(dz=3)),
    ]
    pass_to_core(14)
    pass_to_core(6)
    for copy in kv_x_far:
        copy.wait_recv()
    pass_to_core(10)
    for copy in kv_core:
        copy.wait_recv()

    att_copies = []
    wo_core = {}
    for h in range(HEADS_DEV):
        cols = slice(h * HD, h * HD + HD)
        run_max[...] = jnp.full_like(run_max, -1e30)
        run_sum[...] = jnp.zeros_like(run_sum)
        run_acc[...] = jnp.zeros_like(run_acc)
        for t in range(2):
            rows = slice(t * TILE, t * TILE + TILE)
            score[0, rows] = dot_nt(q[h, rows], kv[0, 0, :, cols])

        def body(i, carry):
            for u in range(2):
                slot = 2 * i + u
                after = jnp.minimum(slot + 1, 15)
                for t in range(2):
                    rows = slice(t * TILE, t * TILE + TILE)
                    score[1 - u, rows] = dot_nt(q[h, rows], kv[after, 0, :, cols])
                    now = score[u, rows]
                    high = now[:, :128]
                    for g in range(1, 4):
                        high = jnp.maximum(high, now[:, g * 128 : g * 128 + 128])
                    old = run_max[rows]
                    new = jnp.maximum(old, jnp.max(high, axis=1, keepdims=True))
                    fade = jnp.exp2((old - new) * EXP_SCALE)
                    tally = run_sum[rows] * fade
                    pieces = []
                    for g in range(4):
                        weight = jnp.exp2((now[:, g * 128 : g * 128 + 128] - new) * EXP_SCALE)
                        tally = tally + weight
                        pieces.append(weight.astype(jnp.bfloat16))
                    weights = jnp.concatenate(pieces, axis=1)
                    run_acc[rows] = run_acc[rows] * fade + dot(weights, kv[slot, 1, :, cols])
                    run_max[rows] = new
                    run_sum[rows] = tally
            return carry

        lax.fori_loop(0, 8, body, 0)
        att[0, :, cols] = (
            run_acc[...] / jnp.sum(run_sum[...], axis=1, keepdims=True)
        ).astype(jnp.bfloat16)
        for r in PEERS:
            att_copies.append(
                (mirrored(r), ship(att.at[0, :, cols], att.at[mirrored(r), :, cols], place(rel=r)))
            )
        if h == 0:
            for r in PEERS:
                wo_copies[r].wait_recv()
                wo_core[r] = ship(wo.at[r, half], wo.at[r, half], place(dcore=1))

    load_wo.wait()
    for r in (0,) + PEERS[::-1]:
        if r:
            for rel, copy in att_copies:
                if rel == r:
                    copy.wait_recv()
            wo_core[r].wait_recv()
        for t in range(2):
            rows = slice(t * TILE, t * TILE + TILE)
            term = dot(att[r, rows], wo[r]).astype(jnp.bfloat16).astype(jnp.float32)
            if r == 0:
                total[rows] = term
            else:
                total[rows] += term
    gate = modulation[2:3, own_cols]
    out[...] = (hid[0].astype(jnp.float32) + gate * total[...]).astype(jnp.bfloat16)
    for copy in copies:
        copy.wait_send()


def local(hidden_in, positions, modulation, w_qkv, qk_gain, w_out, stale_kv):
    half_dim = HD // 2
    inverse_freq = 10000.0 ** (-2.0 * jnp.arange(half_dim, dtype=jnp.float32) / HD)
    angles = positions.astype(jnp.float32)[:, None] * jnp.concatenate([inverse_freq] * 2)[None, :]
    vmem = pl.BlockSpec(memory_space=pltpu.VMEM)
    hbm = pl.BlockSpec(memory_space=pl.ANY)
    f32, bf16 = jnp.float32, jnp.bfloat16
    copies = 100
    return pl.pallas_call(
        kernel,
        out_shape=jax.ShapeDtypeStruct((ROWS, COLS), bf16),
        in_specs=[hbm, vmem, vmem, hbm, vmem, hbm, hbm],
        out_specs=vmem,
        scratch_shapes=[
            pltpu.VMEM((8, ROWS, COLS), bf16),
            pltpu.VMEM((3, MODEL, WIDTH), bf16),
            pltpu.VMEM((16, 2, ROWS, WIDTH), bf16),
            pltpu.VMEM((8, WIDTH, COLS), bf16),
            pltpu.VMEM((8, ROWS, WIDTH), bf16),
            pltpu.VMEM((ROWS, 3 * WIDTH), f32),
            pltpu.VMEM((HEADS_DEV, ROWS, HD), bf16),
            pltpu.VMEM((ROWS, HD), f32),
            pltpu.VMEM((ROWS, HD), f32),
            pltpu.VMEM((ROWS, 128), f32),
            pltpu.VMEM((ROWS, 128), f32),
            pltpu.VMEM((8, 8, ROWS), f32),
            pltpu.VMEM((8, 8, ROWS), f32),
            pltpu.VMEM((8, ROWS), f32),
            pltpu.VMEM((8, ROWS), f32),
            pltpu.VMEM((ROWS, 128), f32),
            pltpu.VMEM((ROWS, 128), f32),
            pltpu.VMEM((ROWS, HD), f32),
            pltpu.VMEM((2, ROWS, ROWS), f32),
            pltpu.VMEM((ROWS, COLS), f32),
            pltpu.SemaphoreType.DMA((copies,)),
            pltpu.SemaphoreType.DMA((copies,)),
            pltpu.SemaphoreType.DMA((3,)),
        ],
        compiler_params=pltpu.CompilerParams(
            collective_id=0, has_side_effects=True, vmem_limit_bytes=60 << 20
        ),
        cost_estimate=pl.CostEstimate(
            flops=15_000_000_000, bytes_accessed=40_000_000, transcendentals=13_000_000
        ),
        name="attention_sublayer",
    )(
        hidden_in, angles, modulation, jnp.transpose(w_qkv, (1, 0, 2)), qk_gain, w_out,
        jnp.transpose(stale_kv, (1, 0, 2)),
    )


def solution(mesh):
    return jax.shard_map(
        local,
        mesh=mesh,
        in_specs=(
            P("patch", "head"),
            P("patch"),
            P(),
            P(None, None, "head"),
            P(None, "head"),
            P("head", None),
            P("patch", None, "head"),
        ),
        out_specs=P("patch", "head"),
        check_vma=False,
    )
```

```python
import functools
import math

import jax
import jax.numpy as jnp
from jax import lax
from jax.experimental import pallas as pl
from jax.experimental.pallas import tpu as pltpu
from jax.sharding import PartitionSpec as P

HD = 128
HEADS_DEV = 3
MODEL = 5120
COLS = 640
ROWS = 512
WIDTH = 384
FULL = 3072
TILE = 256
EXP_SCALE = HD ** (-0.5) * math.log2(math.e)
MESH = pl.DeviceIdType.MESH
NT = (((1,), (1,)), ((), ()))
PEERS = (6, 2, 5, 7, 1, 3, 4)
WO_SLOT = (0, 1, 4, 2, 3, 5, 6, 7)
ORDER = (
    (0, 0, 1), (1, 0, 0), (1, 0, 1), (3, 0, 0), (3, 0, 1), (2, 0, 0), (2, 0, 1), (0, 1, 0),
    (0, 1, 1), (1, 1, 0), (1, 1, 1), (3, 1, 0), (3, 1, 1), (2, 1, 0), (2, 1, 1), (0, 0, 0),
)
SLOT = {where: i for i, where in enumerate(ORDER)}
OWN = SLOT[0, 0, 0]


def dot(left, right):
    return jnp.dot(left, right, preferred_element_type=jnp.float32)


def dot_nt(left, right):
    return lax.dot_general(left, right, NT, preferred_element_type=jnp.float32)


def mirrored(rel):
    return 4 * (rel // 4) + (4 - rel % 4) % 4


def to_rows(first, second):
    lane = lax.broadcasted_iota(jnp.int32, (first.shape[0], 128), 1)
    wide = jnp.where(lane == 0, first, jnp.where(lane == 1, second, 0.0))
    return wide.T[:8]


def to_columns(first, second):
    n = first.shape[1]
    sub = lax.broadcasted_iota(jnp.int32, (128, n), 0)
    tall = jnp.where(sub == 0, first, jnp.where(sub == 1, second, 0.0)).T
    return (
        jnp.broadcast_to(tall[:, 0:1], (n, 128)),
        jnp.broadcast_to(tall[:, 1:2], (n, 128)),
    )


def kernel(
    hid_in, places, freq, modulation, w_in, gain, wout_in, kv_in, out,
    hid, w, kv, wo, att, acc, q, cosine, sine, mean, rstd, stats, norms,
    own_stats, own_norms, run_max, run_sum, run_acc, score, total, send, recv, local,
):
    patch, head = lax.axis_index("patch"), lax.axis_index("head")
    z, xh, core = patch // 4, (patch // 2) % 2, patch % 2
    xl, y = head // 4, head % 4
    count = [0]
    copies = []

    def place(dz=0, dxh=0, dcore=0, rel=0):
        to_patch = ((z + dz) % 4) * 4 + ((xh + dxh) % 2) * 2 + (core + dcore) % 2
        to_head = ((xl + rel // 4) % 2) * 4 + (y + rel % 4) % 4
        return (to_patch, to_head)

    def ship(src, dst, to):
        i = count[0]
        count[0] += 1
        copy = pltpu.make_async_remote_copy(
            src_ref=src, dst_ref=dst, send_sem=send.at[i], recv_sem=recv.at[i],
            device_id=to, device_id_type=MESH,
        )
        copy.start()
        copies.append(copy)
        return copy

    def arrive(*these):
        for copy in these:
            copy.wait_recv()

    load_hid = pltpu.make_async_copy(hid_in, hid.at[0], local.at[0])
    load_hid.start()
    load_w = pltpu.make_async_copy(w_in, w, local.at[1])
    load_w.start()
    own_cols = pl.ds(pl.multiple_of(head * COLS, COLS), COLS)
    load_wo = pltpu.make_async_copy(wout_in.at[:, own_cols], wo.at[0], local.at[2])
    load_wo.start()

    partners = [place(rel=r) for r in PEERS]
    partners += [place(dz=1), place(dz=3), place(dxh=1), place(dcore=1)]
    barrier = pltpu.get_barrier_semaphore()
    for to in partners:
        pl.semaphore_signal(barrier, inc=1, device_id=to, device_id_type=MESH)
    pl.semaphore_wait(barrier, len(partners))

    part = lambda t: pl.ds(t * TILE, TILE)
    low = lambda t: pl.ds(t * TILE, TILE // 2)
    high = lambda t: pl.ds(t * TILE + TILE // 2, TILE // 2)

    def spread(buffer, source, t):
        return {
            rel: ship(source.at[part(t)], buffer.at[mirrored(rel), part(t)], place(rel=rel))
            for rel in (1, 3, 4)
        }

    def relay(buffer, near, t):
        arrive(near[1], near[3])
        far = (
            ship(buffer.at[3, low(t)], buffer.at[2, low(t)], place(rel=1)),
            ship(buffer.at[1, high(t)], buffer.at[2, high(t)], place(rel=3)),
        )
        arrive(near[4])
        side = (
            ship(buffer.at[4, part(t)], buffer.at[7, part(t)], place(rel=1)),
            ship(buffer.at[4, part(t)], buffer.at[5, part(t)], place(rel=3)),
        )
        return far, side

    def across_y(buffer, far, side, t):
        arrive(*far, *side)
        return (
            ship(buffer.at[7, low(t)], buffer.at[6, low(t)], place(rel=1)),
            ship(buffer.at[5, high(t)], buffer.at[6, high(t)], place(rel=3)),
        )

    def pass_to_core(where):
        here, there = SLOT[where + (0,)], SLOT[where + (1,)]
        return ship(kv.at[here], kv.at[there], place(dcore=1))

    near, far, side, opp = {}, {}, {}, {}
    near[0] = spread(hid, hid_in, 0)
    kv_z = {dz: ship(kv_in, kv.at[SLOT[(4 - dz) % 4, 0, 0]], place(dz=dz)) for dz in (1, 3)}
    kv_core = {(0, 0): ship(kv_in, kv.at[SLOT[0, 0, 1]], place(dcore=1))}

    load_hid.wait()
    own = hid[0].astype(jnp.float32)
    own_sum = jnp.sum(own, axis=1, keepdims=True)
    off = own - own_sum * (1.0 / COLS)
    own_stats[...] = to_rows(own_sum, jnp.sum(off * off, axis=1, keepdims=True))
    stat_copies = [ship(own_stats, stats.at[mirrored(r)], place(rel=r)) for r in PEERS]
    stats[0] = own_stats[...]

    spots = places[...].astype(jnp.float32)
    angles = to_columns(spots, spots)[0] * freq[...]
    lane = lax.broadcasted_iota(jnp.int32, (ROWS, HD), 1)
    cosine[...] = jnp.cos(angles)
    sine[...] = jnp.where(lane < HD // 2, -1.0, 1.0) * jnp.sin(angles)

    arrive(*stat_copies)
    sums = sum(stats[r, 0:1, :] for r in range(8))
    mean_row = sums * (1.0 / MODEL)
    squares = sum(
        stats[r, 1:2, :] + COLS * jnp.square(stats[r, 0:1, :] * (1.0 / COLS) - mean_row)
        for r in range(8)
    )
    mean[...], rstd[...] = to_columns(mean_row, lax.rsqrt(squares * (1.0 / MODEL) + 1e-6))
    load_w.wait()

    def project(rel, t):
        rows = slice(t * TILE, t * TILE + TILE)
        block = ((xl + rel // 4) % 2) * 4 + (y + rel % 4) % 4
        at = pl.ds(pl.multiple_of(block * COLS, COLS), COLS)
        features = hid[rel, rows].astype(jnp.float32)
        centre = jnp.concatenate([mean[rows]] * (COLS // 128), axis=1)
        factor = jnp.concatenate([rstd[rows]] * (COLS // 128), axis=1)
        shift, scale = modulation[0:1, at], modulation[1:2, at]
        modulated = ((features - centre) * factor * (1.0 + scale) + shift).astype(jnp.bfloat16)
        for j in range(3):
            cols = slice(j * WIDTH, j * WIDTH + WIDTH)
            term = dot(modulated, w[j, at, :])
            if rel == 0:
                acc[rows, cols] = term
            else:
                acc[rows, cols] += term

    def send_norms(t):
        rows = slice(t * TILE, t * TILE + TILE)
        queries, keys = acc[rows, :WIDTH], acc[rows, WIDTH : 2 * WIDTH]
        own_norms[t] = to_rows(
            jnp.sum(queries * queries, axis=1, keepdims=True),
            jnp.sum(keys * keys, axis=1, keepdims=True),
        )
        norms[t, 0] = own_norms[t]
        return [ship(own_norms.at[t], norms.at[t, mirrored(r)], place(rel=r)) for r in PEERS]

    def finish_projection(t, norm_copies):
        rows = slice(t * TILE, t * TILE + TILE)
        kv[OWN, 1, rows] = acc[rows, 2 * WIDTH :].astype(jnp.bfloat16)
        arrive(*norm_copies)
        factors = to_columns(
            *(
                lax.rsqrt(sum(norms[t, r, i : i + 1, :] for r in range(8)) * (1.0 / FULL) + 1e-6)
                for i in range(2)
            )
        )
        for h in range(HEADS_DEV):
            for i, factor in enumerate(factors):
                cols = slice(h * HD, h * HD + HD)
                value = acc[rows, i * WIDTH + h * HD : i * WIDTH + h * HD + HD]
                value = value * factor * gain[i : i + 1, cols]
                turned = value * cosine[rows] + pltpu.roll(value, HD // 2, 1) * sine[rows]
                if i == 0:
                    q[h, rows] = turned.astype(jnp.bfloat16)
                else:
                    kv[OWN, 0, rows, cols] = turned.astype(jnp.bfloat16)

    def attend(t, first, slots):
        rows = slice(t * TILE, t * TILE + TILE)
        columns = [slice(h * HD, h * HD + HD) for h in range(HEADS_DEV)]
        for h, cols in enumerate(columns):
            if first == 0:
                run_max[h, rows] = jnp.full((TILE, 128), -1e30, jnp.float32)
                run_sum[h, rows] = jnp.zeros((TILE, 128), jnp.float32)
                run_acc[h, rows] = jnp.zeros((TILE, HD), jnp.float32)
            score[0, h] = dot_nt(q[h, rows], kv[first, 0, :, cols])

        def body(i, carry):
            for u in range(2):
                slot = first + 2 * i + u
                after = jnp.minimum(slot + 1, first + slots - 1)
                for h, cols in enumerate(columns):
                    score[1 - u, h] = dot_nt(q[h, rows], kv[after, 0, :, cols])
                    now = score[u, h]
                    peak = now[:, :128]
                    for g in range(1, 4):
                        peak = jnp.maximum(peak, now[:, g * 128 : g * 128 + 128])
                    old = run_max[h, rows]
                    new = jnp.maximum(old, jnp.max(peak, axis=1, keepdims=True))
                    fade = jnp.exp2((old - new) * EXP_SCALE)
                    tally = run_sum[h, rows] * fade
                    pieces = []
                    for g in range(4):
                        weight = jnp.exp2((now[:, g * 128 : g * 128 + 128] - new) * EXP_SCALE)
                        tally = tally + weight
                        pieces.append(weight.astype(jnp.bfloat16))
                    weights = jnp.concatenate(pieces, axis=1)
                    run_acc[h, rows] = run_acc[h, rows] * fade + dot(weights, kv[slot, 1, :, cols])
                    run_max[h, rows] = new
                    run_sum[h, rows] = tally
            return carry

        lax.fori_loop(0, slots // 2, body, 0)

    def publish(t):
        rows = slice(t * TILE, t * TILE + TILE)
        for h in range(HEADS_DEV):
            att[0, rows, h * HD : h * HD + HD] = (
                run_acc[h, rows] / jnp.sum(run_sum[h, rows], axis=1, keepdims=True)
            ).astype(jnp.bfloat16)
        return spread(att, att.at[0], t)

    def across_x(far, t):
        arrive(*far)
        return ship(att.at[2, part(t)], att.at[6, part(t)], place(rel=4))

    def output(r, t):
        rows = slice(t * TILE, t * TILE + TILE)
        term = dot(att[r, rows], wo[WO_SLOT[r]]).astype(jnp.bfloat16).astype(jnp.float32)
        if r == 0:
            total[rows] = term
        else:
            total[rows] += term

    for t in range(2):
        project(0, t)
    far[0], side[0] = relay(hid, near[0], 0)
    kv_x = ship(kv_in, kv.at[SLOT[0, 1, 0]], place(dxh=1))
    for rel in (1, 3, 4):
        project(rel, 0)
    arrive(kv_z[1], kv_z[3])
    up, down, two = SLOT[3, 0, 0], SLOT[1, 0, 0], SLOT[2, 0, 0]
    kv_far = (
        ship(kv.at[up, 0], kv.at[two, 0], place(dz=1)),
        ship(kv.at[down, 1], kv.at[two, 1], place(dz=3)),
    )
    kv_core[3, 0], kv_core[1, 0] = pass_to_core((3, 0)), pass_to_core((1, 0))
    opp[0] = across_y(hid, far[0], side[0], 0)
    for rel in (2, 5, 7):
        project(rel, 0)
    near[1] = spread(hid, hid_in, 1)
    arrive(*opp[0])
    project(6, 0)
    norm_copies = send_norms(0)
    arrive(*kv_far)
    kv_core[2, 0] = pass_to_core((2, 0))
    kv_x_far = ship(kv.at[two], kv.at[SLOT[2, 1, 0]], place(dxh=1))
    arrive(kv_x)
    beside = SLOT[0, 1, 0]
    kv_x_z = (
        ship(kv.at[beside], kv.at[SLOT[3, 1, 0]], place(dz=1)),
        ship(kv.at[beside], kv.at[SLOT[1, 1, 0]], place(dz=3)),
    )
    kv_core[0, 1] = pass_to_core((0, 1))
    finish_projection(0, norm_copies)
    far[1], side[1] = relay(hid, near[1], 1)
    for rel in (1, 3, 4):
        project(rel, 1)
    arrive(kv_core[0, 0], kv_core[1, 0], kv_core[3, 0], kv_core[2, 0])
    attend(0, 0, 8)
    opp[1] = across_y(hid, far[1], side[1], 1)
    for rel in (2, 5, 7):
        project(rel, 1)
    HALF, EIGHTH = WIDTH // 2, WIDTH // 8
    half = pl.ds(pl.multiple_of(core * HALF, HALF), HALF)
    share = lambda dz: pl.ds(
        pl.multiple_of((((z + dz) % 4) * 2 + core) * EIGHTH, EIGHTH), EIGHTH
    )
    arrive(*opp[1])
    project(6, 1)
    norm_copies = send_norms(1)
    wo_copies = []
    for r in PEERS:
        to = place(rel=r)
        rows = half if r in (1, 3, 4) else share(0)
        cols = pl.ds(pl.multiple_of(to[1] * COLS, COLS), COLS)
        wo_copies.append(ship(wout_in.at[rows, cols], wo.at[WO_SLOT[mirrored(r)], rows], to))
    arrive(*kv_x_z)
    kv_core[3, 1], kv_core[1, 1] = pass_to_core((3, 1)), pass_to_core((1, 1))
    arrive(kv_x_far)
    kv_core[2, 1] = pass_to_core((2, 1))
    finish_projection(1, norm_copies)
    attend(1, 0, 8)
    arrive(*wo_copies)
    wo_z = [ship(wo.at[4:8, share(0)], wo.at[4:8, share(0)], place(dz=dz)) for dz in (1, 3)]
    wo_core = [
        ship(wo.at[1:4, half], wo.at[1:4, half], place(dcore=1)),
        ship(wo.at[4:8, share(0)], wo.at[4:8, share(0)], place(dcore=1)),
    ]
    arrive(kv_core[0, 1], kv_core[1, 1], kv_core[3, 1], kv_core[2, 1])
    attend(0, 8, 8)
    att_near = {0: publish(0)}
    att_far, att_side, att_opp = {}, {}, {}
    attend(1, 8, 4)
    att_far[0], att_side[0] = relay(att, att_near[0], 0)
    arrive(*wo_z)
    wo_far = (
        ship(wo.at[4:6, share(3)], wo.at[4:6, share(3)], place(dz=1)),
        ship(wo.at[6:8, share(1)], wo.at[6:8, share(1)], place(dz=3)),
    )
    for dz in (1, 3):
        wo_core.append(ship(wo.at[4:8, share(dz)], wo.at[4:8, share(dz)], place(dcore=1)))
    attend(1, 12, 4)
    att_near[1] = publish(1)
    att_opp[0] = across_x(att_far[0], 0)
    arrive(*wo_far)
    wo_core.append(ship(wo.at[4:8, share(2)], wo.at[4:8, share(2)], place(dcore=1)))
    load_wo.wait()
    output(0, 0)
    output(0, 1)
    att_far[1], att_side[1] = relay(att, att_near[1], 1)
    arrive(*wo_core)
    for r in (1, 3, 4, 2):
        output(r, 0)
    att_opp[1] = across_x(att_far[1], 1)
    arrive(*att_side[0], att_opp[0])
    for r in (5, 7, 6):
        output(r, 0)
    for r in (1, 3, 4, 2):
        output(r, 1)
    arrive(*att_side[1])
    output(5, 1)
    output(7, 1)
    arrive(att_opp[1])
    output(6, 1)
    gate = modulation[2:3, own_cols]
    out[...] = (hid[0].astype(jnp.float32) + gate * total[...]).astype(jnp.bfloat16)
    for copy in copies:
        copy.wait_send()


def local(hidden_in, positions, modulation, w_qkv, qk_gain, w_out, stale_kv):
    half_dim = HD // 2
    inverse_freq = 10000.0 ** (-2.0 * jnp.arange(half_dim, dtype=jnp.float32) / HD)
    frequencies = jnp.concatenate([inverse_freq] * 2)[None, :]
    vmem = pl.BlockSpec(memory_space=pltpu.VMEM)
    hbm = pl.BlockSpec(memory_space=pl.ANY)
    f32, bf16 = jnp.float32, jnp.bfloat16
    copies = 100
    return pl.pallas_call(
        kernel,
        out_shape=jax.ShapeDtypeStruct((ROWS, COLS), bf16),
        in_specs=[hbm, vmem, vmem, vmem, hbm, vmem, hbm, hbm],
        out_specs=vmem,
        scratch_shapes=[
            pltpu.VMEM((8, ROWS, COLS), bf16),
            pltpu.VMEM((3, MODEL, WIDTH), bf16),
            pltpu.VMEM((16, 2, ROWS, WIDTH), bf16),
            pltpu.VMEM((8, WIDTH, COLS), bf16),
            pltpu.VMEM((8, ROWS, WIDTH), bf16),
            pltpu.VMEM((ROWS, 3 * WIDTH), f32),
            pltpu.VMEM((HEADS_DEV, ROWS, HD), bf16),
            pltpu.VMEM((ROWS, HD), f32),
            pltpu.VMEM((ROWS, HD), f32),
            pltpu.VMEM((ROWS, 128), f32),
            pltpu.VMEM((ROWS, 128), f32),
            pltpu.VMEM((8, 8, ROWS), f32),
            pltpu.VMEM((2, 8, 8, TILE), f32),
            pltpu.VMEM((8, ROWS), f32),
            pltpu.VMEM((2, 8, TILE), f32),
            pltpu.VMEM((HEADS_DEV, ROWS, 128), f32),
            pltpu.VMEM((HEADS_DEV, ROWS, 128), f32),
            pltpu.VMEM((HEADS_DEV, ROWS, HD), f32),
            pltpu.VMEM((2, HEADS_DEV, TILE, ROWS), f32),
            pltpu.VMEM((ROWS, COLS), f32),
            pltpu.SemaphoreType.DMA((copies,)),
            pltpu.SemaphoreType.DMA((copies,)),
            pltpu.SemaphoreType.DMA((3,)),
        ],
        compiler_params=pltpu.CompilerParams(
            collective_id=0, has_side_effects=True, vmem_limit_bytes=60 << 20
        ),
        cost_estimate=pl.CostEstimate(
            flops=15_000_000_000, bytes_accessed=40_000_000, transcendentals=13_000_000
        ),
        name="attention_sublayer",
    )(
        hidden_in, positions[None, :], frequencies, modulation, jnp.transpose(w_qkv, (1, 0, 2)), qk_gain, w_out,
        jnp.transpose(stale_kv, (1, 0, 2)),
    )


def solution(mesh):
    return jax.shard_map(
        local,
        mesh=mesh,
        in_specs=(
            P("patch", "head"),
            P("patch"),
            P(),
            P(None, None, "head"),
            P(None, "head"),
            P("head", None),
            P("patch", None, "head"),
        ),
        out_specs=P("patch", "head"),
        check_vma=False,
    )
```

```python
import functools
import math

import jax
import jax.numpy as jnp
from jax import lax
from jax.experimental import pallas as pl
from jax.experimental.pallas import tpu as pltpu
from jax.sharding import PartitionSpec as P

HD = 128
HEADS_DEV = 3
MODEL = 5120
COLS = 640
ROWS = 512
WIDTH = 384
FULL = 3072
TILE = 256
EXP_SCALE = HD ** (-0.5) * math.log2(math.e)
MESH = pl.DeviceIdType.MESH
NT = (((1,), (1,)), ((), ()))
PEERS = (6, 2, 5, 7, 4, 1, 3)
WO_SLOT = (0, 1, 4, 2, 3, 5, 6, 7)
NEAR, FAR = 5, slice(3, 8)
ORDER = (
    (0, 0, 1), (1, 0, 0), (1, 0, 1), (3, 0, 0), (3, 0, 1), (2, 0, 0), (2, 0, 1), (0, 1, 0),
    (0, 1, 1), (1, 1, 0), (1, 1, 1), (3, 1, 0), (3, 1, 1), (2, 1, 0), (2, 1, 1), (0, 0, 0),
)
SLOT = {where: i for i, where in enumerate(ORDER)}
OWN = SLOT[0, 0, 0]


def dot(left, right):
    return jnp.dot(left, right, preferred_element_type=jnp.float32)


def dot_nt(left, right):
    return lax.dot_general(left, right, NT, preferred_element_type=jnp.float32)


def mirrored(rel):
    return 4 * (rel // 4) + (4 - rel % 4) % 4


def to_rows(first, second):
    lane = lax.broadcasted_iota(jnp.int32, (first.shape[0], 128), 1)
    wide = jnp.where(lane == 0, first, jnp.where(lane == 1, second, 0.0))
    return wide.T[:8]


def to_columns(first, second):
    n = first.shape[1]
    sub = lax.broadcasted_iota(jnp.int32, (128, n), 0)
    tall = jnp.where(sub == 0, first, jnp.where(sub == 1, second, 0.0)).T
    return (
        jnp.broadcast_to(tall[:, 0:1], (n, 128)),
        jnp.broadcast_to(tall[:, 1:2], (n, 128)),
    )


def kernel(
    hid_in, places, freq, modulation, w_in, gain, wout_in, kv_in, out,
    hid, w, kv, wo, att, acc, q, cosine, sine, mean, rstd, stats, norms,
    own_stats, own_norms, run_max, run_sum, run_acc, score, total, send, recv, local,
):
    patch, head = lax.axis_index("patch"), lax.axis_index("head")
    z, xh, core = patch // 4, (patch // 2) % 2, patch % 2
    xl, y = head // 4, head % 4
    count = [0]
    copies = []

    def place(dz=0, dxh=0, dcore=0, rel=0):
        to_patch = ((z + dz) % 4) * 4 + ((xh + dxh) % 2) * 2 + (core + dcore) % 2
        to_head = ((xl + rel // 4) % 2) * 4 + (y + rel % 4) % 4
        return (to_patch, to_head)

    def ship(src, dst, to):
        i = count[0]
        count[0] += 1
        copy = pltpu.make_async_remote_copy(
            src_ref=src, dst_ref=dst, send_sem=send.at[i], recv_sem=recv.at[i],
            device_id=to, device_id_type=MESH,
        )
        copy.start()
        copies.append(copy)
        return copy

    def arrive(*these):
        for copy in these:
            copy.wait_recv()

    load_hid = pltpu.make_async_copy(hid_in, hid.at[0], local.at[0])
    load_hid.start()
    load_w = pltpu.make_async_copy(w_in, w, local.at[1])
    load_w.start()
    own_cols = pl.ds(pl.multiple_of(head * COLS, COLS), COLS)
    load_wo = pltpu.make_async_copy(wout_in.at[:, own_cols], wo.at[0], local.at[2])
    load_wo.start()

    partners = [place(rel=r) for r in PEERS]
    partners += [place(dz=1), place(dz=3), place(dxh=1), place(dcore=1)]
    barrier = pltpu.get_barrier_semaphore()
    for to in partners:
        pl.semaphore_signal(barrier, inc=1, device_id=to, device_id_type=MESH)
    pl.semaphore_wait(barrier, len(partners))

    part = lambda t: pl.ds(t * TILE, TILE)
    low = lambda t: pl.ds(t * TILE, TILE // 2)
    high = lambda t: pl.ds(t * TILE + TILE // 2, TILE // 2)

    every = slice(None)

    def spread(buffer, source, t, cols=every):
        return {
            rel: ship(
                source.at[part(t), cols], buffer.at[mirrored(rel), part(t), cols], place(rel=rel)
            )
            for rel in (4, 1, 3)
        }

    def onward(buffer, near, t, cols=every):
        arrive(near[1], near[3])
        return (
            ship(buffer.at[3, low(t), cols], buffer.at[2, low(t), cols], place(rel=1)),
            ship(buffer.at[1, high(t), cols], buffer.at[2, high(t), cols], place(rel=3)),
        )

    def sideways(buffer, near, t, cols=every):
        arrive(near[4])
        return (
            ship(buffer.at[4, part(t), cols], buffer.at[7, part(t), cols], place(rel=1)),
            ship(buffer.at[4, part(t), cols], buffer.at[5, part(t), cols], place(rel=3)),
        )

    def across_y(buffer, side, t):
        arrive(*side)
        return (
            ship(buffer.at[7, low(t)], buffer.at[6, low(t)], place(rel=1)),
            ship(buffer.at[5, high(t)], buffer.at[6, high(t)], place(rel=3)),
        )

    def pass_to_core(where):
        here, there = SLOT[where + (0,)], SLOT[where + (1,)]
        return ship(kv.at[here], kv.at[there], place(dcore=1))

    near, far, side, opp = {}, {}, {}, {}
    near[0] = spread(hid, hid_in, 0)
    kv_z = {dz: ship(kv_in, kv.at[SLOT[(4 - dz) % 4, 0, 0]], place(dz=dz)) for dz in (1, 3)}
    kv_core = {(0, 0): ship(kv_in, kv.at[SLOT[0, 0, 1]], place(dcore=1))}

    load_hid.wait()
    own = hid[0].astype(jnp.float32)
    own_sum = jnp.sum(own, axis=1, keepdims=True)
    off = own - own_sum * (1.0 / COLS)
    own_stats[...] = to_rows(own_sum, jnp.sum(off * off, axis=1, keepdims=True))
    stat_copies = [ship(own_stats, stats.at[mirrored(r)], place(rel=r)) for r in PEERS]
    stats[0] = own_stats[...]

    spots = places[...].astype(jnp.float32)
    angles = to_columns(spots, spots)[0] * freq[...]
    lane = lax.broadcasted_iota(jnp.int32, (ROWS, HD), 1)
    cosine[...] = jnp.cos(angles)
    sine[...] = jnp.where(lane < HD // 2, -1.0, 1.0) * jnp.sin(angles)

    far[0] = onward(hid, near[0], 0)
    side[0] = sideways(hid, near[0], 0)
    near[1] = spread(hid, hid_in, 1)
    kv_x = ship(kv_in, kv.at[SLOT[0, 1, 0]], place(dxh=1))

    arrive(*stat_copies)
    sums = sum(stats[r, 0:1, :] for r in range(8))
    mean_row = sums * (1.0 / MODEL)
    squares = sum(
        stats[r, 1:2, :] + COLS * jnp.square(stats[r, 0:1, :] * (1.0 / COLS) - mean_row)
        for r in range(8)
    )
    mean[...], rstd[...] = to_columns(mean_row, lax.rsqrt(squares * (1.0 / MODEL) + 1e-6))
    load_w.wait()

    def project(rel, t):
        rows = slice(t * TILE, t * TILE + TILE)
        block = ((xl + rel // 4) % 2) * 4 + (y + rel % 4) % 4
        at = pl.ds(pl.multiple_of(block * COLS, COLS), COLS)
        features = hid[rel, rows].astype(jnp.float32)
        centre = jnp.concatenate([mean[rows]] * (COLS // 128), axis=1)
        factor = jnp.concatenate([rstd[rows]] * (COLS // 128), axis=1)
        shift, scale = modulation[0:1, at], modulation[1:2, at]
        modulated = ((features - centre) * factor * (1.0 + scale) + shift).astype(jnp.bfloat16)
        for j in range(3):
            cols = slice(j * WIDTH, j * WIDTH + WIDTH)
            term = dot(modulated, w[j, at, :])
            if rel == 0:
                acc[rows, cols] = term
            else:
                acc[rows, cols] += term

    def send_norms(t):
        rows = slice(t * TILE, t * TILE + TILE)
        queries, keys = acc[rows, :WIDTH], acc[rows, WIDTH : 2 * WIDTH]
        own_norms[t] = to_rows(
            jnp.sum(queries * queries, axis=1, keepdims=True),
            jnp.sum(keys * keys, axis=1, keepdims=True),
        )
        norms[t, 0] = own_norms[t]
        return [ship(own_norms.at[t], norms.at[t, mirrored(r)], place(rel=r)) for r in PEERS]

    def finish_projection(t, norm_copies):
        rows = slice(t * TILE, t * TILE + TILE)
        kv[OWN, 1, rows] = acc[rows, 2 * WIDTH :].astype(jnp.bfloat16)
        arrive(*norm_copies)
        factors = to_columns(
            *(
                lax.rsqrt(sum(norms[t, r, i : i + 1, :] for r in range(8)) * (1.0 / FULL) + 1e-6)
                for i in range(2)
            )
        )
        for h in range(HEADS_DEV):
            for i, factor in enumerate(factors):
                cols = slice(h * HD, h * HD + HD)
                value = acc[rows, i * WIDTH + h * HD : i * WIDTH + h * HD + HD]
                value = value * factor * gain[i : i + 1, cols]
                turned = value * cosine[rows] + pltpu.roll(value, HD // 2, 1) * sine[rows]
                if i == 0:
                    q[h, rows] = turned.astype(jnp.bfloat16)
                else:
                    kv[OWN, 0, rows, cols] = turned.astype(jnp.bfloat16)

    def attend(t, first, slots, heads=tuple(range(HEADS_DEV))):
        rows = slice(t * TILE, t * TILE + TILE)
        columns = [slice(h * HD, h * HD + HD) for h in range(HEADS_DEV)]
        for h in heads:
            cols = columns[h]
            if first == 0:
                run_max[h, rows] = jnp.full((TILE, 128), -1e30, jnp.float32)
                run_sum[h, rows] = jnp.zeros((TILE, 128), jnp.float32)
                run_acc[h, rows] = jnp.zeros((TILE, HD), jnp.float32)
            score[0, h] = dot_nt(q[h, rows], kv[first, 0, :, cols])

        def body(i, carry):
            for u in range(2):
                slot = first + 2 * i + u
                after = jnp.minimum(slot + 1, first + slots - 1)
                for h in heads:
                    cols = columns[h]
                    score[1 - u, h] = dot_nt(q[h, rows], kv[after, 0, :, cols])
                    now = score[u, h]
                    peak = now[:, :128]
                    for g in range(1, 4):
                        peak = jnp.maximum(peak, now[:, g * 128 : g * 128 + 128])
                    old = run_max[h, rows]
                    new = jnp.maximum(old, jnp.max(peak, axis=1, keepdims=True))
                    fade = jnp.exp2((old - new) * EXP_SCALE)
                    tally = run_sum[h, rows] * fade
                    pieces = []
                    for g in range(4):
                        weight = jnp.exp2((now[:, g * 128 : g * 128 + 128] - new) * EXP_SCALE)
                        tally = tally + weight
                        pieces.append(weight.astype(jnp.bfloat16))
                    weights = jnp.concatenate(pieces, axis=1)
                    run_acc[h, rows] = run_acc[h, rows] * fade + dot(weights, kv[slot, 1, :, cols])
                    run_max[h, rows] = new
                    run_sum[h, rows] = tally
            return carry

        lax.fori_loop(0, slots // 2, body, 0)

    def publish(t, heads):
        rows = slice(t * TILE, t * TILE + TILE)
        for h in heads:
            att[0, rows, h * HD : h * HD + HD] = (
                run_acc[h, rows] / jnp.sum(run_sum[h, rows], axis=1, keepdims=True)
            ).astype(jnp.bfloat16)
        return spread(att, att.at[0], t, span(heads))

    def span(heads):
        return slice(heads[0] * HD, heads[-1] * HD + HD)

    def across_x(far, t, cols=every):
        arrive(*far)
        return ship(att.at[2, part(t), cols], att.at[6, part(t), cols], place(rel=4))

    def output(r, t):
        rows = slice(t * TILE, t * TILE + TILE)
        term = dot(att[r, rows], wo[WO_SLOT[r]]).astype(jnp.bfloat16).astype(jnp.float32)
        if r == 0:
            total[rows] = term
        else:
            total[rows] += term

    for t in range(2):
        project(0, t)
    for rel in (1, 3, 4):
        project(rel, 0)
    arrive(*far[0])
    project(2, 0)
    arrive(kv_z[1], kv_z[3])
    up, down, two = SLOT[3, 0, 0], SLOT[1, 0, 0], SLOT[2, 0, 0]
    kv_far = (
        ship(kv.at[up, 0], kv.at[two, 0], place(dz=1)),
        ship(kv.at[down, 1], kv.at[two, 1], place(dz=3)),
    )
    kv_core[3, 0], kv_core[1, 0] = pass_to_core((3, 0)), pass_to_core((1, 0))
    far[1] = onward(hid, near[1], 1)
    opp[0] = across_y(hid, side[0], 0)
    side[1] = sideways(hid, near[1], 1)
    for rel in (5, 7):
        project(rel, 0)
    arrive(kv_x)
    beside = SLOT[0, 1, 0]
    kv_x_z = (
        ship(kv.at[beside], kv.at[SLOT[3, 1, 0]], place(dz=1)),
        ship(kv.at[beside], kv.at[SLOT[1, 1, 0]], place(dz=3)),
    )
    kv_core[0, 1] = pass_to_core((0, 1))
    for rel in (1, 3, 4):
        project(rel, 1)
    arrive(*kv_far)
    kv_core[2, 0] = pass_to_core((2, 0))
    kv_x_far = [ship(kv.at[two, 0], kv.at[SLOT[2, 1, 0], 0], place(dxh=1))]
    arrive(*opp[0])
    project(6, 0)
    norm_copies = send_norms(0)
    arrive(*far[1])
    project(2, 1)
    opp[1] = across_y(hid, side[1], 1)
    finish_projection(0, norm_copies)
    HALF, EIGHTH = WIDTH // 2, WIDTH // 8
    half = pl.ds(pl.multiple_of(core * HALF, HALF), HALF)
    share = lambda dz: pl.ds(
        pl.multiple_of((((z + dz) % 4) * 2 + core) * EIGHTH, EIGHTH), EIGHTH
    )

    def send_weights(r, rows):
        to = place(rel=r)
        cols = pl.ds(pl.multiple_of(to[1] * COLS, COLS), COLS)
        return ship(wout_in.at[rows, cols], wo.at[WO_SLOT[mirrored(r)], rows], to)

    wo_copies = [send_weights(r, share(0)) for r in PEERS[:NEAR]]
    arrive(kv_core[0, 0], kv_core[1, 0], kv_core[3, 0], kv_core[2, 0])
    attend(0, 0, 8)
    for rel in (5, 7):
        project(rel, 1)
    arrive(*opp[1])
    project(6, 1)
    norm_copies = send_norms(1)
    arrive(*kv_x_z)
    above, below, last = SLOT[3, 1, 0], SLOT[1, 1, 0], SLOT[2, 1, 0]
    kv_x_far += [
        ship(kv.at[above, 1, part(0)], kv.at[last, 1, part(0)], place(dz=1)),
        ship(kv.at[below, 1, part(1)], kv.at[last, 1, part(1)], place(dz=3)),
    ]
    kv_core[3, 1], kv_core[1, 1] = pass_to_core((3, 1)), pass_to_core((1, 1))
    finish_projection(1, norm_copies)
    wo_copies += [send_weights(r, half) for r in PEERS[NEAR:]]
    attend(1, 0, 8)
    arrive(*kv_x_far)
    kv_core[2, 1] = pass_to_core((2, 1))
    arrive(*wo_copies[:NEAR])
    wo_z = [ship(wo.at[FAR, share(0)], wo.at[FAR, share(0)], place(dz=dz)) for dz in (1, 3)]
    wo_core = [ship(wo.at[FAR, share(0)], wo.at[FAR, share(0)], place(dcore=1))]
    arrive(kv_core[0, 1], kv_core[1, 1], kv_core[3, 1], kv_core[2, 1])
    parts = ((0, (0, 1)), (0, (2,)), (1, (0, 1)), (1, (2,)))
    att_near, att_far, att_side, att_opp = {}, {}, {}, {}

    def attend_and_publish(i):
        t, heads = parts[i]
        attend(t, 8, 8, heads)
        att_near[i] = publish(t, heads)

    def first_relay(i):
        t, heads = parts[i]
        att_far[i] = onward(att, att_near[i], t, span(heads))
        att_side[i] = sideways(att, att_near[i], t, span(heads))

    def second_relay(i):
        t, heads = parts[i]
        att_opp[i] = across_x(att_far[i], t, span(heads))

    attend_and_publish(0)
    attend_and_publish(1)
    first_relay(0)
    attend_and_publish(2)
    first_relay(1)
    second_relay(0)
    arrive(*wo_copies[NEAR:])
    wo_core.append(ship(wo.at[1:3, half], wo.at[1:3, half], place(dcore=1)))
    arrive(*wo_z)
    wo_far = (
        ship(wo.at[3:5, share(3)], wo.at[3:5, share(3)], place(dz=1)),
        ship(wo.at[5:8, share(1)], wo.at[5:8, share(1)], place(dz=3)),
    )
    for dz in (1, 3):
        wo_core.append(ship(wo.at[FAR, share(dz)], wo.at[FAR, share(dz)], place(dcore=1)))
    attend_and_publish(3)
    first_relay(2)
    second_relay(1)
    load_wo.wait()
    output(0, 0)
    output(0, 1)
    arrive(*wo_far)
    wo_core.append(ship(wo.at[FAR, share(2)], wo.at[FAR, share(2)], place(dcore=1)))
    first_relay(3)
    second_relay(2)
    arrive(wo_core[1])
    for r in (1, 3):
        output(r, 0)
        output(r, 1)
    second_relay(3)
    arrive(wo_core[0], *wo_core[2:])
    for r in (4, 2):
        output(r, 0)
        output(r, 1)
    arrive(*att_side[0], *att_side[1], att_opp[0], att_opp[1])
    for r in (5, 7, 6):
        output(r, 0)
    arrive(*att_side[2], *att_side[3])
    output(5, 1)
    output(7, 1)
    arrive(att_opp[2], att_opp[3])
    output(6, 1)
    gate = modulation[2:3, own_cols]
    out[...] = (hid[0].astype(jnp.float32) + gate * total[...]).astype(jnp.bfloat16)
    for copy in copies:
        copy.wait_send()


def local(hidden_in, positions, modulation, w_qkv, qk_gain, w_out, stale_kv):
    half_dim = HD // 2
    inverse_freq = 10000.0 ** (-2.0 * jnp.arange(half_dim, dtype=jnp.float32) / HD)
    frequencies = jnp.concatenate([inverse_freq] * 2)[None, :]
    vmem = pl.BlockSpec(memory_space=pltpu.VMEM)
    hbm = pl.BlockSpec(memory_space=pl.ANY)
    f32, bf16 = jnp.float32, jnp.bfloat16
    copies = 120
    return pl.pallas_call(
        kernel,
        out_shape=jax.ShapeDtypeStruct((ROWS, COLS), bf16),
        in_specs=[hbm, vmem, vmem, vmem, hbm, vmem, hbm, hbm],
        out_specs=vmem,
        scratch_shapes=[
            pltpu.VMEM((8, ROWS, COLS), bf16),
            pltpu.VMEM((3, MODEL, WIDTH), bf16),
            pltpu.VMEM((16, 2, ROWS, WIDTH), bf16),
            pltpu.VMEM((8, WIDTH, COLS), bf16),
            pltpu.VMEM((8, ROWS, WIDTH), bf16),
            pltpu.VMEM((ROWS, 3 * WIDTH), f32),
            pltpu.VMEM((HEADS_DEV, ROWS, HD), bf16),
            pltpu.VMEM((ROWS, HD), f32),
            pltpu.VMEM((ROWS, HD), f32),
            pltpu.VMEM((ROWS, 128), f32),
            pltpu.VMEM((ROWS, 128), f32),
            pltpu.VMEM((8, 8, ROWS), f32),
            pltpu.VMEM((2, 8, 8, TILE), f32),
            pltpu.VMEM((8, ROWS), f32),
            pltpu.VMEM((2, 8, TILE), f32),
            pltpu.VMEM((HEADS_DEV, ROWS, 128), f32),
            pltpu.VMEM((HEADS_DEV, ROWS, 128), f32),
            pltpu.VMEM((HEADS_DEV, ROWS, HD), f32),
            pltpu.VMEM((2, HEADS_DEV, TILE, ROWS), f32),
            pltpu.VMEM((ROWS, COLS), f32),
            pltpu.SemaphoreType.DMA((copies,)),
            pltpu.SemaphoreType.DMA((copies,)),
            pltpu.SemaphoreType.DMA((3,)),
        ],
        compiler_params=pltpu.CompilerParams(
            collective_id=0, has_side_effects=True, vmem_limit_bytes=60 << 20
        ),
        cost_estimate=pl.CostEstimate(
            flops=15_000_000_000, bytes_accessed=40_000_000, transcendentals=13_000_000
        ),
        name="attention_sublayer",
    )(
        hidden_in, positions[None, :], frequencies, modulation, jnp.transpose(w_qkv, (1, 0, 2)), qk_gain, w_out,
        jnp.transpose(stale_kv, (1, 0, 2)),
    )


def solution(mesh):
    return jax.shard_map(
        local,
        mesh=mesh,
        in_specs=(
            P("patch", "head"),
            P("patch"),
            P(),
            P(None, None, "head"),
            P(None, "head"),
            P("head", None),
            P("patch", None, "head"),
        ),
        out_specs=P("patch", "head"),
        check_vma=False,
    )
```

```python
import functools
import math

import jax
import jax.numpy as jnp
from jax import lax
from jax.experimental import pallas as pl
from jax.experimental.pallas import tpu as pltpu
from jax.sharding import PartitionSpec as P

HD = 128
HEADS_DEV = 3
MODEL = 5120
COLS = 640
ROWS = 512
WIDTH = 384
FULL = 3072
TILE = 256
EXP_SCALE = HD ** (-0.5) * math.log2(math.e)
MESH = pl.DeviceIdType.MESH
NT = (((1,), (1,)), ((), ()))
PEERS = (6, 2, 5, 7, 4, 1, 3)
WO_SLOT = (0, 1, 4, 2, 3, 5, 6, 7)
NEAR, FAR = 5, slice(3, 8)
ORDER = (
    (0, 0, 1), (1, 0, 0), (1, 0, 1), (3, 0, 0), (3, 0, 1), (2, 0, 0), (2, 0, 1), (0, 1, 0),
    (0, 1, 1), (1, 1, 0), (1, 1, 1), (3, 1, 0), (3, 1, 1), (2, 1, 0), (2, 1, 1), (0, 0, 0),
)
SLOT = {where: i for i, where in enumerate(ORDER)}
OWN = SLOT[0, 0, 0]


def dot(left, right):
    return jnp.dot(left, right, preferred_element_type=jnp.float32)


def dot_nt(left, right):
    return lax.dot_general(left, right, NT, preferred_element_type=jnp.float32)


def mirrored(rel):
    return 4 * (rel // 4) + (4 - rel % 4) % 4


def to_rows(first, second):
    lane = lax.broadcasted_iota(jnp.int32, (first.shape[0], 128), 1)
    wide = jnp.where(lane == 0, first, jnp.where(lane == 1, second, 0.0))
    return wide.T[:8]


def to_columns(first, second):
    n = first.shape[1]
    sub = lax.broadcasted_iota(jnp.int32, (128, n), 0)
    tall = jnp.where(sub == 0, first, jnp.where(sub == 1, second, 0.0)).T
    return (
        jnp.broadcast_to(tall[:, 0:1], (n, 128)),
        jnp.broadcast_to(tall[:, 1:2], (n, 128)),
    )


def kernel(
    hid_in, places, freq, modulation, w_in, gain, wout_in, kv_in, out,
    hid, w, kv, wo, att, acc, q, cosine, sine, mean, rstd, stats, norms,
    own_stats, own_norms, run_max, run_sum, run_acc, score, total, send, recv, local,
):
    patch, head = lax.axis_index("patch"), lax.axis_index("head")
    z, xh, core = patch // 4, (patch // 2) % 2, patch % 2
    xl, y = head // 4, head % 4
    count = [0]
    copies = []

    def place(dz=0, dxh=0, dcore=0, rel=0):
        to_patch = ((z + dz) % 4) * 4 + ((xh + dxh) % 2) * 2 + (core + dcore) % 2
        to_head = ((xl + rel // 4) % 2) * 4 + (y + rel % 4) % 4
        return (to_patch, to_head)

    def ship(src, dst, to):
        i = count[0]
        count[0] += 1
        copy = pltpu.make_async_remote_copy(
            src_ref=src, dst_ref=dst, send_sem=send.at[i], recv_sem=recv.at[i],
            device_id=to, device_id_type=MESH,
        )
        copy.start()
        copies.append(copy)
        return copy

    def arrive(*these):
        for copy in these:
            copy.wait_recv()

    load_hid = pltpu.make_async_copy(hid_in, hid.at[0], local.at[0])
    load_hid.start()
    load_w = pltpu.make_async_copy(w_in, w, local.at[1])
    load_w.start()
    own_cols = pl.ds(pl.multiple_of(head * COLS, COLS), COLS)
    load_wo = pltpu.make_async_copy(wout_in.at[:, own_cols], wo.at[0], local.at[2])
    load_wo.start()

    partners = [place(rel=r) for r in PEERS]
    partners += [place(dz=1), place(dz=3), place(dxh=1), place(dcore=1)]
    barrier = pltpu.get_barrier_semaphore()
    for to in partners:
        pl.semaphore_signal(barrier, inc=1, device_id=to, device_id_type=MESH)
    pl.semaphore_wait(barrier, len(partners))

    part = lambda t: pl.ds(t * TILE, TILE)
    low = lambda t: pl.ds(t * TILE, TILE // 2)
    high = lambda t: pl.ds(t * TILE + TILE // 2, TILE // 2)

    every = slice(None)

    def spread(buffer, source, t, cols=every):
        return {
            rel: ship(
                source.at[part(t), cols], buffer.at[mirrored(rel), part(t), cols], place(rel=rel)
            )
            for rel in (4, 1, 3)
        }

    def onward(buffer, near, t, cols=every):
        arrive(near[1], near[3])
        return (
            ship(buffer.at[3, low(t), cols], buffer.at[2, low(t), cols], place(rel=1)),
            ship(buffer.at[1, high(t), cols], buffer.at[2, high(t), cols], place(rel=3)),
        )

    def sideways(buffer, near, t, cols=every):
        arrive(near[4])
        return (
            ship(buffer.at[4, part(t), cols], buffer.at[7, part(t), cols], place(rel=1)),
            ship(buffer.at[4, part(t), cols], buffer.at[5, part(t), cols], place(rel=3)),
        )

    def across_y(buffer, side, t):
        arrive(*side)
        return (
            ship(buffer.at[7, low(t)], buffer.at[6, low(t)], place(rel=1)),
            ship(buffer.at[5, high(t)], buffer.at[6, high(t)], place(rel=3)),
        )

    def pass_to_core(where):
        here, there = SLOT[where + (0,)], SLOT[where + (1,)]
        return ship(kv.at[here], kv.at[there], place(dcore=1))

    near, far, side, opp = {}, {}, {}, {}
    near[0] = spread(hid, hid_in, 0)
    kv_z = {dz: ship(kv_in, kv.at[SLOT[(4 - dz) % 4, 0, 0]], place(dz=dz)) for dz in (1, 3)}
    kv_core = {(0, 0): ship(kv_in, kv.at[SLOT[0, 0, 1]], place(dcore=1))}

    load_hid.wait()
    own = hid[0].astype(jnp.float32)
    own_sum = jnp.sum(own, axis=1, keepdims=True)
    off = own - own_sum * (1.0 / COLS)
    own_stats[...] = to_rows(own_sum, jnp.sum(off * off, axis=1, keepdims=True))
    stat_copies = [ship(own_stats, stats.at[mirrored(r)], place(rel=r)) for r in PEERS]
    stats[0] = own_stats[...]

    spots = places[...].astype(jnp.float32)
    angles = to_columns(spots, spots)[0] * freq[...]
    lane = lax.broadcasted_iota(jnp.int32, (ROWS, HD), 1)
    cosine[...] = jnp.cos(angles)
    sine[...] = jnp.where(lane < HD // 2, -1.0, 1.0) * jnp.sin(angles)

    far[0] = onward(hid, near[0], 0)
    side[0] = sideways(hid, near[0], 0)
    near[1] = spread(hid, hid_in, 1)
    kv_x = ship(kv_in, kv.at[SLOT[0, 1, 0]], place(dxh=1))

    arrive(*stat_copies)
    sums = sum(stats[r, 0:1, :] for r in range(8))
    mean_row = sums * (1.0 / MODEL)
    squares = sum(
        stats[r, 1:2, :] + COLS * jnp.square(stats[r, 0:1, :] * (1.0 / COLS) - mean_row)
        for r in range(8)
    )
    mean[...], rstd[...] = to_columns(mean_row, lax.rsqrt(squares * (1.0 / MODEL) + 1e-6))
    load_w.wait()

    def project(rel, t):
        rows = slice(t * TILE, t * TILE + TILE)
        block = ((xl + rel // 4) % 2) * 4 + (y + rel % 4) % 4
        at = pl.ds(pl.multiple_of(block * COLS, COLS), COLS)
        features = hid[rel, rows].astype(jnp.float32)
        centre = jnp.concatenate([mean[rows]] * (COLS // 128), axis=1)
        factor = jnp.concatenate([rstd[rows]] * (COLS // 128), axis=1)
        shift, scale = modulation[0:1, at], modulation[1:2, at]
        modulated = ((features - centre) * factor * (1.0 + scale) + shift).astype(jnp.bfloat16)
        for j in range(3):
            cols = slice(j * WIDTH, j * WIDTH + WIDTH)
            term = dot(modulated, w[j, at, :])
            if rel == 0:
                acc[rows, cols] = term
            else:
                acc[rows, cols] += term

    def send_norms(t):
        rows = slice(t * TILE, t * TILE + TILE)
        queries, keys = acc[rows, :WIDTH], acc[rows, WIDTH : 2 * WIDTH]
        own_norms[t] = to_rows(
            jnp.sum(queries * queries, axis=1, keepdims=True),
            jnp.sum(keys * keys, axis=1, keepdims=True),
        )
        norms[t, 0] = own_norms[t]
        return [ship(own_norms.at[t], norms.at[t, mirrored(r)], place(rel=r)) for r in PEERS]

    def finish_projection(t, norm_copies):
        rows = slice(t * TILE, t * TILE + TILE)
        kv[OWN, 1, rows] = acc[rows, 2 * WIDTH :].astype(jnp.bfloat16)
        arrive(*norm_copies)
        factors = to_columns(
            *(
                lax.rsqrt(sum(norms[t, r, i : i + 1, :] for r in range(8)) * (1.0 / FULL) + 1e-6)
                for i in range(2)
            )
        )
        for h in range(HEADS_DEV):
            for i, factor in enumerate(factors):
                cols = slice(h * HD, h * HD + HD)
                value = acc[rows, i * WIDTH + h * HD : i * WIDTH + h * HD + HD]
                value = value * factor * gain[i : i + 1, cols]
                turned = value * cosine[rows] + pltpu.roll(value, HD // 2, 1) * sine[rows]
                if i == 0:
                    q[h, rows] = turned.astype(jnp.bfloat16)
                else:
                    kv[OWN, 0, rows, cols] = turned.astype(jnp.bfloat16)

    def attend(t, first, slots, heads=tuple(range(HEADS_DEV))):
        rows = slice(t * TILE, t * TILE + TILE)
        columns = [slice(h * HD, h * HD + HD) for h in range(HEADS_DEV)]
        for h in heads:
            cols = columns[h]
            if first == 0:
                run_max[h, rows] = jnp.full((TILE, 128), -1e30, jnp.float32)
                run_sum[h, rows] = jnp.zeros((TILE, 128), jnp.float32)
                run_acc[h, rows] = jnp.zeros((TILE, HD), jnp.float32)
            for e in range(2):
                score[0, h, e] = dot_nt(q[h, rows], kv[first + e, 0, :, cols])

        def body(i, carry):
            for u in range(2):
                slot = first + 4 * i + 2 * u
                after = jnp.minimum(slot + 2, first + slots - 2)
                for h in heads:
                    cols = columns[h]
                    for e in range(2):
                        score[1 - u, h, e] = dot_nt(q[h, rows], kv[after + e, 0, :, cols])
                    now = [
                        score[u, h, e, :, g * 128 : g * 128 + 128]
                        for e in range(2)
                        for g in range(4)
                    ]
                    peak = functools.reduce(jnp.maximum, now)
                    old = run_max[h, rows]
                    new = jnp.maximum(old, jnp.max(peak, axis=1, keepdims=True))
                    fade = jnp.exp2((old - new) * EXP_SCALE)
                    weights = [jnp.exp2((piece - new) * EXP_SCALE) for piece in now]
                    run_sum[h, rows] = run_sum[h, rows] * fade + sum(weights)
                    rounded = [piece.astype(jnp.bfloat16) for piece in weights]
                    gained = sum(
                        dot(jnp.concatenate(rounded[4 * e : 4 * e + 4], axis=1), kv[slot + e, 1, :, cols])
                        for e in range(2)
                    )
                    run_acc[h, rows] = run_acc[h, rows] * fade + gained
                    run_max[h, rows] = new
            return carry

        lax.fori_loop(0, slots // 4, body, 0)

    def publish(t, heads):
        rows = slice(t * TILE, t * TILE + TILE)
        for h in heads:
            att[0, rows, h * HD : h * HD + HD] = (
                run_acc[h, rows] / jnp.sum(run_sum[h, rows], axis=1, keepdims=True)
            ).astype(jnp.bfloat16)
        return spread(att, att.at[0], t, span(heads))

    def span(heads):
        return slice(heads[0] * HD, heads[-1] * HD + HD)

    def across_x(far, t, cols=every):
        arrive(*far)
        return ship(att.at[2, part(t), cols], att.at[6, part(t), cols], place(rel=4))

    def output(r, t):
        rows = slice(t * TILE, t * TILE + TILE)
        term = dot(att[r, rows], wo[WO_SLOT[r]]).astype(jnp.bfloat16).astype(jnp.float32)
        if r == 0:
            total[rows] = term
        else:
            total[rows] += term

    def finish(t):
        rows = slice(t * TILE, t * TILE + TILE)
        gate = modulation[2:3, own_cols]
        out[rows] = (hid[0, rows].astype(jnp.float32) + gate * total[rows]).astype(jnp.bfloat16)

    for t in range(2):
        project(0, t)
    for rel in (1, 3, 4):
        project(rel, 0)
    arrive(*far[0])
    project(2, 0)
    arrive(kv_z[1], kv_z[3])
    up, down, two = SLOT[3, 0, 0], SLOT[1, 0, 0], SLOT[2, 0, 0]
    kv_far = (
        ship(kv.at[up, 0], kv.at[two, 0], place(dz=1)),
        ship(kv.at[down, 1], kv.at[two, 1], place(dz=3)),
    )
    kv_core[3, 0], kv_core[1, 0] = pass_to_core((3, 0)), pass_to_core((1, 0))
    far[1] = onward(hid, near[1], 1)
    opp[0] = across_y(hid, side[0], 0)
    side[1] = sideways(hid, near[1], 1)
    for rel in (5, 7):
        project(rel, 0)
    arrive(kv_x)
    beside = SLOT[0, 1, 0]
    kv_x_z = (
        ship(kv.at[beside], kv.at[SLOT[3, 1, 0]], place(dz=1)),
        ship(kv.at[beside], kv.at[SLOT[1, 1, 0]], place(dz=3)),
    )
    kv_core[0, 1] = pass_to_core((0, 1))
    for rel in (1, 3, 4):
        project(rel, 1)
    arrive(*kv_far)
    kv_core[2, 0] = pass_to_core((2, 0))
    kv_x_far = [ship(kv.at[two, 0], kv.at[SLOT[2, 1, 0], 0], place(dxh=1))]
    arrive(*opp[0])
    project(6, 0)
    norm_copies = send_norms(0)
    arrive(*far[1])
    project(2, 1)
    opp[1] = across_y(hid, side[1], 1)
    finish_projection(0, norm_copies)
    HALF, EIGHTH = WIDTH // 2, WIDTH // 8
    half = pl.ds(pl.multiple_of(core * HALF, HALF), HALF)
    share = lambda dz: pl.ds(
        pl.multiple_of((((z + dz) % 4) * 2 + core) * EIGHTH, EIGHTH), EIGHTH
    )

    def send_weights(r, rows):
        to = place(rel=r)
        cols = pl.ds(pl.multiple_of(to[1] * COLS, COLS), COLS)
        return ship(wout_in.at[rows, cols], wo.at[WO_SLOT[mirrored(r)], rows], to)

    wo_copies = [send_weights(r, share(0)) for r in PEERS[:NEAR]]
    arrive(kv_core[0, 0], kv_core[1, 0], kv_core[3, 0], kv_core[2, 0])
    attend(0, 0, 8)
    for rel in (5, 7):
        project(rel, 1)
    arrive(*opp[1])
    project(6, 1)
    norm_copies = send_norms(1)
    arrive(*kv_x_z)
    above, below, last = SLOT[3, 1, 0], SLOT[1, 1, 0], SLOT[2, 1, 0]
    kv_x_far += [
        ship(kv.at[above, 1, part(0)], kv.at[last, 1, part(0)], place(dz=1)),
        ship(kv.at[below, 1, part(1)], kv.at[last, 1, part(1)], place(dz=3)),
    ]
    kv_core[3, 1], kv_core[1, 1] = pass_to_core((3, 1)), pass_to_core((1, 1))
    finish_projection(1, norm_copies)
    wo_copies += [send_weights(r, half) for r in PEERS[NEAR:]]
    attend(1, 0, 8)
    arrive(*kv_x_far)
    kv_core[2, 1] = pass_to_core((2, 1))
    arrive(*wo_copies[:NEAR])
    wo_z = [ship(wo.at[FAR, share(0)], wo.at[FAR, share(0)], place(dz=dz)) for dz in (1, 3)]
    wo_core = [ship(wo.at[FAR, share(0)], wo.at[FAR, share(0)], place(dcore=1))]
    arrive(kv_core[0, 1], kv_core[1, 1], kv_core[3, 1], kv_core[2, 1])
    parts = ((0, (0, 1)), (0, (2,)), (1, (0, 1)), (1, (2,)))
    att_near, att_far, att_side, att_opp = {}, {}, {}, {}

    def attend_and_publish(i):
        t, heads = parts[i]
        attend(t, 8, 8, heads)
        att_near[i] = publish(t, heads)

    def first_relay(i):
        t, heads = parts[i]
        att_far[i] = onward(att, att_near[i], t, span(heads))
        att_side[i] = sideways(att, att_near[i], t, span(heads))

    def second_relay(i):
        t, heads = parts[i]
        att_opp[i] = across_x(att_far[i], t, span(heads))

    attend_and_publish(0)
    attend_and_publish(1)
    first_relay(0)
    attend_and_publish(2)
    first_relay(1)
    second_relay(0)
    arrive(*wo_copies[NEAR:])
    wo_core.append(ship(wo.at[1:3, half], wo.at[1:3, half], place(dcore=1)))
    arrive(*wo_z)
    wo_far = (
        ship(wo.at[3:5, share(3)], wo.at[3:5, share(3)], place(dz=1)),
        ship(wo.at[5:8, share(1)], wo.at[5:8, share(1)], place(dz=3)),
    )
    for dz in (1, 3):
        wo_core.append(ship(wo.at[FAR, share(dz)], wo.at[FAR, share(dz)], place(dcore=1)))
    attend_and_publish(3)
    first_relay(2)
    second_relay(1)
    load_wo.wait()
    output(0, 0)
    output(0, 1)
    arrive(*wo_far)
    wo_core.append(ship(wo.at[FAR, share(2)], wo.at[FAR, share(2)], place(dcore=1)))
    first_relay(3)
    second_relay(2)
    arrive(wo_core[1])
    for r in (1, 3):
        output(r, 0)
        output(r, 1)
    second_relay(3)
    arrive(wo_core[0], *wo_core[2:])
    for r in (4, 2):
        output(r, 0)
        output(r, 1)
    arrive(*att_side[0], *att_side[1], att_opp[0], att_opp[1])
    for r in (5, 7, 6):
        output(r, 0)
    finish(0)
    arrive(*att_side[2], *att_side[3])
    output(5, 1)
    output(7, 1)
    arrive(att_opp[2], att_opp[3])
    output(6, 1)
    finish(1)
    for copy in copies:
        copy.wait_send()


def local(hidden_in, positions, modulation, w_qkv, qk_gain, w_out, stale_kv):
    half_dim = HD // 2
    inverse_freq = 10000.0 ** (-2.0 * jnp.arange(half_dim, dtype=jnp.float32) / HD)
    frequencies = jnp.concatenate([inverse_freq] * 2)[None, :]
    vmem = pl.BlockSpec(memory_space=pltpu.VMEM)
    hbm = pl.BlockSpec(memory_space=pl.ANY)
    f32, bf16 = jnp.float32, jnp.bfloat16
    copies = 120
    return pl.pallas_call(
        kernel,
        out_shape=jax.ShapeDtypeStruct((ROWS, COLS), bf16),
        in_specs=[hbm, vmem, vmem, vmem, hbm, vmem, hbm, hbm],
        out_specs=vmem,
        scratch_shapes=[
            pltpu.VMEM((8, ROWS, COLS), bf16),
            pltpu.VMEM((3, MODEL, WIDTH), bf16),
            pltpu.VMEM((16, 2, ROWS, WIDTH), bf16),
            pltpu.VMEM((8, WIDTH, COLS), bf16),
            pltpu.VMEM((8, ROWS, WIDTH), bf16),
            pltpu.VMEM((ROWS, 3 * WIDTH), f32),
            pltpu.VMEM((HEADS_DEV, ROWS, HD), bf16),
            pltpu.VMEM((ROWS, HD), f32),
            pltpu.VMEM((ROWS, HD), f32),
            pltpu.VMEM((ROWS, 128), f32),
            pltpu.VMEM((ROWS, 128), f32),
            pltpu.VMEM((8, 8, ROWS), f32),
            pltpu.VMEM((2, 8, 8, TILE), f32),
            pltpu.VMEM((8, ROWS), f32),
            pltpu.VMEM((2, 8, TILE), f32),
            pltpu.VMEM((HEADS_DEV, ROWS, 128), f32),
            pltpu.VMEM((HEADS_DEV, ROWS, 128), f32),
            pltpu.VMEM((HEADS_DEV, ROWS, HD), f32),
            pltpu.VMEM((2, HEADS_DEV, 2, TILE, ROWS), f32),
            pltpu.VMEM((ROWS, COLS), f32),
            pltpu.SemaphoreType.DMA((copies,)),
            pltpu.SemaphoreType.DMA((copies,)),
            pltpu.SemaphoreType.DMA((3,)),
        ],
        compiler_params=pltpu.CompilerParams(
            collective_id=0, has_side_effects=True, vmem_limit_bytes=60 << 20
        ),
        cost_estimate=pl.CostEstimate(
            flops=15_000_000_000, bytes_accessed=40_000_000, transcendentals=13_000_000
        ),
        name="attention_sublayer",
    )(
        hidden_in, positions[None, :], frequencies, modulation, jnp.transpose(w_qkv, (1, 0, 2)), qk_gain, w_out,
        jnp.transpose(stale_kv, (1, 0, 2)),
    )


def solution(mesh):
    return jax.shard_map(
        local,
        mesh=mesh,
        in_specs=(
            P("patch", "head"),
            P("patch"),
            P(),
            P(None, None, "head"),
            P(None, "head"),
            P("head", None),
            P("patch", None, "head"),
        ),
        out_specs=P("patch", "head"),
        check_vma=False,
    )
```
